32 devices in a mesh: sec: 2 (over y), col: 4 (over z), row: 4 (over x, core).
Axes of the slice: x: 2, y: 2, z: 4, core: 2. Of those that a mesh axis runs over, the one named last changes fastest.
Arguments:
- ancestor: float32 [16384, 16384], P('row', ('sec', 'col')), may hold values from -0.3 to 0.3
- panel: float32 [2, 8192, 2048], P('sec', 'row', 'col'), may hold values from -1.5 to 1.5
- diag_inverse: float32 [2, 2048, 2048], P('sec', 'col', 'row'), may hold values from -12 to 12
- frontier: int32 [2, 16, 4], replicated, may hold values from 0 to 7, as said below
- counts: int32 [2, 16], replicated, may hold values from 1 to 4
- pattern: int32 [2, 64, 64], replicated, may hold values 0 or 1
Outputs:
- cross_block: float32 [2, 2048, 8192], P('sec', 'col', 'row')
- inverse: float32 [2, 2048, 2048], P('sec', 'col', 'row')
The draws below stay inside these ranges and needn't reach their ends.
Inputs may be any that keep to these rules, and one draw needn't show every extreme that they name: The 4 offsets of one child and group are distinct; slot j of group g is ancestor tile 8 * g + frontier[c, g, j]. Slots j >= counts[c, g] of group g are padding for child c.
All inputs are finite; a program needn't handle non-finite values.
Results may differ from the reference program's by a relative error of at most 0.0001.
Values sent between devices are 32-bit elements; how exact they have to be, the bound alone decides.
A program may use at most 256 MiB of HBM per device.

```python
import jax
import jax.numpy as jnp
from jax import lax

ORDER = 16384
PANEL = 2048
TILE = 128
GROUP = 8
SLOTS = 4
GROUPS = 16
FSLOTS = 64
FRONT = 8192


def draw_frontier(key, part):
    scores = jax.random.randint(key, (2, GROUPS, GROUP), 0, 1 << 20)
    scores = scores * GROUP + jnp.arange(GROUP, dtype=jnp.int32)
    ordering = jnp.argsort(scores, axis=-1, stable=True)
    return ordering[:, :, :SLOTS].astype(jnp.int32)


def place_ends(array, rng, low, top_value):
    longest = array.shape.index(max(array.shape))
    spots = []
    for shift in (0, 1):
        where = [jax.random.randint(jax.random.fold_in(rng, axis), (), 0, length) for axis, length in enumerate(array.shape)]
        where[longest] = (where[longest] + shift) % array.shape[longest]
        spots.append(tuple(where))
    return array.at[spots[0]].set(low).at[spots[1]].set(top_value)


def level_of(key, shape, cuts, smallest, largest):
    def one(axis_at, parts):
        heights = jax.random.uniform(jax.random.fold_in(jax.random.fold_in(key, 6), axis_at), (parts,), jnp.float32, smallest / len(cuts), largest / len(cuts))
        return jnp.repeat(jnp.exp(heights), shape[axis_at] // parts).reshape((-1,) + (1,) * (len(shape) - axis_at - 1))

    gain = one(*cuts[0])
    for cut in cuts[1:]:
        gain = gain * one(*cut)
    return gain


def centred(stream_key, dims, scale, limit, split=(), kind=jnp.bfloat16):
    drawn = scale * jax.random.normal(stream_key, dims, jnp.float32)
    if split:
        drawn = drawn * level_of(stream_key, dims, split, -0.22, 0.18)
    return jnp.clip(drawn, -limit, limit).astype(kind)


def setup_inputs(seed: int = 0) -> dict:
    seeds = jax.random.split(jax.random.key(seed), 7)
    return {
        "ancestor": centred(seeds[0], (ORDER, ORDER), 0.05, 0.3, ((0, 4), (1, 8)), jnp.float32),
        "panel": centred(seeds[1], (2, FRONT, PANEL), 0.25, 1.5, ((0, 2), (1, 4), (2, 4)), jnp.float32),
        "diag_inverse": centred(seeds[2], (2, PANEL, PANEL), 2.0, 12.0, ((0, 2), (1, 4), (2, 4)), jnp.float32),
        "frontier": draw_frontier(jax.random.fold_in(seeds[6], 71), 0),
        "counts": place_ends(jax.random.randint(seeds[4], (2, GROUPS), 1, SLOTS + 1), jax.random.fold_in(seeds[4], 1), 1, SLOTS).astype(jnp.int32),
        "pattern": place_ends((jax.random.randint(seeds[5], (2, FSLOTS, FSLOTS), 0, 5) < 3).astype(jnp.int32), jax.random.fold_in(seeds[5], 1), 0, 1),
    }


def reference(ancestor, panel, diag_inverse, frontier, counts, pattern):
    cross_list = []
    inverse_list = []
    for child_id in range(2):
        slot_ids = jnp.arange(SLOTS).astype(jnp.int32)
        group_ids = jnp.arange(GROUPS).astype(jnp.int32)
        tile_ids = (group_ids[:, None] * GROUP + frontier[child_id].astype(jnp.int32)).reshape(-1)
        alive_slots = (slot_ids[None, :] < counts[child_id][:, None]).reshape(-1).astype(jnp.float32)
        within = jnp.arange(TILE).astype(jnp.int32)
        indices = (tile_ids[:, None] * TILE + within[None, :]).reshape(-1)
        picked = jnp.take(jnp.take(ancestor, indices, axis=0), indices, axis=1)
        tile_mask = pattern[child_id].astype(jnp.float32) * alive_slots[:, None] * alive_slots[None, :]
        picked = (picked.reshape(FSLOTS, TILE, FSLOTS, TILE) * tile_mask[:, None, :, None]).reshape(FRONT, FRONT)
        product = jnp.dot(picked, panel[child_id], precision=lax.Precision.HIGHEST, preferred_element_type=jnp.float32)
        cross_part = -product.T
        inverse_part = diag_inverse[child_id] - jnp.dot(cross_part, panel[child_id], precision=lax.Precision.HIGHEST, preferred_element_type=jnp.float32)
        cross_list.append(cross_part)
        inverse_list.append(inverse_part)
    return jnp.stack(cross_list), jnp.stack(inverse_list)
```

```python
import functools

import jax
import jax.numpy as jnp
from jax import lax
from jax.experimental import pallas as pl
from jax.experimental.pallas import tpu as pltpu
from jax.sharding import PartitionSpec as P

TILE = 128
GROUP = 8
SLOTS = 4


def pick_kernel(col_slots, row_tiles, col_tiles, mask, strip, out):
    i = pl.program_id(0)
    for j in range(col_slots):
        start = pl.multiple_of(col_tiles[j] * TILE, TILE)
        tile = strip[:, pl.ds(start, TILE)]
        out[:, j * TILE : (j + 1) * TILE] = jnp.where(mask[i * col_slots + j] != 0, -tile, 0.0)


def pick_tiles(
    ancestor, frontier, counts, pattern, child_id, row_start, block_start, row_groups, block_groups
):
    offsets = lax.dynamic_index_in_dim(frontier, child_id, 0, keepdims=False)
    sizes_live = lax.dynamic_index_in_dim(counts, child_id, 0, keepdims=False)
    pattern_child = lax.dynamic_index_in_dim(pattern, child_id, 0, keepdims=False)
    alive = (jnp.arange(SLOTS, dtype=jnp.int32)[None, :] < sizes_live[:, None]).astype(jnp.int32)
    row_offsets = lax.dynamic_slice_in_dim(offsets, row_start, row_groups, 0)
    col_offsets = lax.dynamic_slice_in_dim(offsets, block_start, block_groups, 0)
    row_tiles = (jnp.arange(row_groups, dtype=jnp.int32)[:, None] * GROUP + row_offsets).reshape(-1)
    col_tiles = (jnp.arange(block_groups, dtype=jnp.int32)[:, None] * GROUP + col_offsets).reshape(
        -1
    )
    row_alive = lax.dynamic_slice_in_dim(alive, row_start, row_groups, 0).reshape(-1)
    col_alive = lax.dynamic_slice_in_dim(alive, block_start, block_groups, 0).reshape(-1)
    row_slots = row_groups * SLOTS
    col_slots = block_groups * SLOTS
    pattern_block = lax.dynamic_slice(
        pattern_child, (row_start * SLOTS, block_start * SLOTS), (row_slots, col_slots)
    )
    mask = (pattern_block * row_alive[:, None] * col_alive[None, :]).reshape(-1)
    width = ancestor.shape[1]
    return pl.pallas_call(
        functools.partial(pick_kernel, col_slots),
        out_shape=jax.ShapeDtypeStruct((row_slots * TILE, col_slots * TILE), jnp.float32),
        grid_spec=pltpu.PrefetchScalarGridSpec(
            num_scalar_prefetch=3,
            grid=(row_slots,),
            in_specs=[pl.BlockSpec((TILE, width), lambda i, rows, cols, kept: (rows[i], 0))],
            out_specs=pl.BlockSpec((TILE, col_slots * TILE), lambda i, rows, cols, kept: (i, 0)),
        ),
        cost_estimate=pl.CostEstimate(
            flops=0,
            bytes_accessed=row_slots * TILE * (width + col_slots * TILE) * 4,
            transcendentals=0,
        ),
    )(row_tiles, col_tiles, mask, ancestor)


def dot_high(left, right, dims):
    return lax.dot_general(
        left,
        right,
        (dims, ((), ())),
        precision=lax.Precision.HIGH,
        preferred_element_type=jnp.float32,
    )


def per_device(ancestor, panel, diag_inverse, frontier, counts, pattern):
    sec_index = lax.axis_index("sec")
    row_index = lax.axis_index("row")
    col_index = lax.axis_index("col")
    row_count = lax.axis_size("row")
    col_count = lax.axis_size("col")
    groups_all = frontier.shape[1]
    row_groups = groups_all // row_count
    block_groups = groups_all // (2 * col_count)
    row_start = row_index * row_groups
    block_start = (sec_index * col_count + col_index) * block_groups
    pick = functools.partial(
        pick_tiles,
        ancestor,
        frontier,
        counts,
        pattern,
        row_start=row_start,
        block_start=block_start,
        row_groups=row_groups,
        block_groups=block_groups,
    )
    theirs = pick(child_id=1 - sec_index)
    partner = lax.ppermute(theirs, "sec", [(0, 1), (1, 0)])
    mine = pick(child_id=sec_index)

    ring = [(c, (c + 1) % col_count) for c in range(col_count)]
    take_rows = block_groups * SLOTS * TILE
    width = panel.shape[2]
    top = row_count // 2
    slot_start = col_index * block_groups % row_groups * SLOTS * TILE
    holders = [c * block_groups // row_groups for c in range(col_count)]
    holder = col_index * block_groups // row_groups
    lead_is_own = ((row_index & top) == 0) == (sec_index == 0)

    def share_in_plane(block):
        part = lax.dynamic_slice_in_dim(block, slot_start, take_rows, 0)
        known = {(c, holders[c] ^ flip) for c in range(col_count) for flip in (0, top)}

        def pairs(bit):
            return sorted((c * row_count + r, c * row_count + (r ^ bit)) for c, r in known)

        other = lax.ppermute(part, ("col", "row"), pairs(top))
        lead = jnp.where(lead_is_own, part, other)
        trail = jnp.where(lead_is_own, other, part)
        bit = top // 2
        while bit:
            got_lead = lax.ppermute(lead, ("col", "row"), pairs(bit))
            got_trail = lax.ppermute(trail, ("col", "row"), pairs(bit))
            fresh = ((row_index ^ holder) & (2 * bit - 1)) == bit
            lead = jnp.where(fresh, got_lead, lead)
            trail = jnp.where(fresh, got_trail, trail)
            known |= {(c, r ^ bit) for c, r in known}
            bit //= 2
        return lead, trail

    blocks = [panel[0]]
    for _ in range(col_count - 1):
        blocks.append(lax.ppermute(blocks[-1], "col", ring))

    def term(block):
        lead, trail = share_in_plane(block)
        return dot_high(lead, mine, ((0,), (1,))) + dot_high(trail, partner, ((0,), (1,)))

    total = term(blocks[1])
    for step in range(2, col_count):
        total = lax.ppermute(total, "col", ring) + term(blocks[step])
    cross_part = lax.ppermute(total, "col", ring) + term(blocks[0])

    rows_full = jnp.zeros((panel.shape[1], width * col_count), jnp.float32)
    for step in range(col_count):
        owner = (col_index - step) % col_count
        rows_full = lax.dynamic_update_slice_in_dim(rows_full, blocks[step], owner * width, 1)
    summed = dot_high(cross_part, rows_full, ((1,), (0,)))
    out_width = diag_inverse.shape[2]
    summed = summed.reshape(width, row_count, out_width)
    bit = 1
    while bit < row_count:
        halves = summed.reshape(width, -1, 2, out_width)
        side = row_index // bit % 2
        kept = lax.dynamic_index_in_dim(halves, side, 2, keepdims=False)
        sent = lax.dynamic_index_in_dim(halves, 1 - side, 2, keepdims=False)
        summed = kept + lax.ppermute(sent, "row", [(r, r ^ bit) for r in range(row_count)])
        bit *= 2
    inverse_part = diag_inverse[0] - summed.reshape(width, out_width)
    return (cross_part[None], inverse_part[None])


def solution(mesh):
    return jax.shard_map(
        per_device,
        mesh=mesh,
        in_specs=(
            P("row", ("sec", "col")),
            P("sec", "row", "col"),
            P("sec", "col", "row"),
            P(),
            P(),
            P(),
        ),
        out_specs=(P("sec", "col", "row"), P("sec", "col", "row")),
        check_vma=False,
    )
```
